32 devices in a mesh: entry: 4 (over y, core), fft: 8 (over z, x).
Axes of the slice: x: 2, y: 2, z: 4, core: 2. Of those that a mesh axis runs over, the one named last changes fastest.
Arguments:
- left_zero_zero: int32 [2048, 4096], P('entry', 'fft'), may hold values from 0 to 65535
- left_zero_one: int32 [2048, 4096], P('entry', 'fft'), may hold values from 0 to 65535
- left_one_zero: int32 [2048, 4096], P('entry', 'fft'), may hold values from 0 to 65535
- left_one_one: int32 [2048, 4096], P('entry', 'fft'), may hold values from 0 to 65535
- right_zero_zero: int32 [2048, 4096], P('entry', 'fft'), may hold values from 0 to 65535
- right_zero_one: int32 [2048, 4096], P('entry', 'fft'), may hold values from 0 to 65535
- right_one_zero: int32 [2048, 4096], P('entry', 'fft'), may hold values from 0 to 65535
- right_one_one: int32 [2048, 4096], P('entry', 'fft'), may hold values from 0 to 65535
Outputs:
- product: float32 [4, 4096, 4096], P('entry', None, 'fft')
The draws below stay inside these ranges and needn't reach their ends.
All inputs are finite; a program needn't handle non-finite values.
Results may differ from the reference program's by a relative error of at most 0.0001.
Values sent between devices are 32-bit elements; how exact they have to be, the bound alone decides.
A program may use at most 384 MiB of HBM per device.

```python
import math
import jax
import jax.numpy as jnp

ROWS = 4096
COLS = 4096
HALF = 2048


def place_ends(drawn, own_key, least, top_value):
    index_at = [jax.random.randint(jax.random.fold_in(own_key, axis), (), 0, length) for axis, length in enumerate(drawn.shape)]
    main_axis = drawn.shape.index(max(drawn.shape))
    beside = index_at[:main_axis] + [(index_at[main_axis] + 1) % drawn.shape[main_axis]] + index_at[main_axis + 1:]
    return drawn.at[tuple(index_at)].set(least).at[tuple(beside)].set(top_value)


def setup_inputs(seed: int = 0) -> dict:
    arg_keys = jax.random.split(jax.random.key(seed), 9)
    left_zero_zero = place_ends(jax.random.randint(arg_keys[0], (HALF, COLS), 0, 65536), jax.random.fold_in(arg_keys[0], 1), 0, 65535).astype(jnp.int32)
    left_zero_one = place_ends(jax.random.randint(arg_keys[1], (HALF, COLS), 0, 65536), jax.random.fold_in(arg_keys[1], 1), 0, 65535).astype(jnp.int32)
    left_one_zero = place_ends(jax.random.randint(arg_keys[2], (HALF, COLS), 0, 65536), jax.random.fold_in(arg_keys[2], 1), 0, 65535).astype(jnp.int32)
    left_one_one = place_ends(jax.random.randint(arg_keys[3], (HALF, COLS), 0, 65536), jax.random.fold_in(arg_keys[3], 1), 0, 65535).astype(jnp.int32)
    right_zero_zero = place_ends(jax.random.randint(arg_keys[4], (HALF, COLS), 0, 65536), jax.random.fold_in(arg_keys[4], 1), 0, 65535).astype(jnp.int32)
    right_zero_one = place_ends(jax.random.randint(arg_keys[5], (HALF, COLS), 0, 65536), jax.random.fold_in(arg_keys[5], 1), 0, 65535).astype(jnp.int32)
    right_one_zero = place_ends(jax.random.randint(arg_keys[6], (HALF, COLS), 0, 65536), jax.random.fold_in(arg_keys[6], 1), 0, 65535).astype(jnp.int32)
    right_one_one = place_ends(jax.random.randint(arg_keys[7], (HALF, COLS), 0, 65536), jax.random.fold_in(arg_keys[7], 1), 0, 65535).astype(jnp.int32)
    return dict(left_zero_zero=left_zero_zero, left_zero_one=left_zero_one, left_one_zero=left_one_zero, left_one_one=left_one_one, right_zero_zero=right_zero_zero, right_zero_one=right_zero_one, right_one_zero=right_one_zero, right_one_one=right_one_one)


def spectrum(limbs, length):
    values = (limbs.astype(jnp.float32) - 32768.0) * (1.0 / 32768.0)
    return jnp.fft.rfft(values.reshape(-1), n=length)

def reference(left_zero_zero, left_zero_one, left_one_zero, left_one_one, right_zero_zero, right_zero_one, right_one_zero, right_one_one):
    length = ROWS * COLS
    lefts = ((spectrum(left_zero_zero, length), spectrum(left_zero_one, length)), (spectrum(left_one_zero, length), spectrum(left_one_one, length)))
    rights = ((spectrum(right_zero_zero, length), spectrum(right_zero_one, length)), (spectrum(right_one_zero, length), spectrum(right_one_one, length)))
    out_scale = 1.0 / math.sqrt(HALF * COLS)
    results = []
    for upper_pick in range(2):
        for lower_pick in range(2):
            mixed = lefts[upper_pick][0] * rights[0][lower_pick] + lefts[upper_pick][1] * rights[1][lower_pick]
            results.append(jnp.fft.irfft(mixed, n=length) * out_scale)
    return jnp.stack(results).reshape(4, ROWS, COLS)
```

```python
import math

import jax
import jax.numpy as jnp
import numpy as np
from jax import lax
from jax.sharding import PartitionSpec as P

LANES = 128
BOTH = ("entry", "fft")
three_pass = lax.Precision.HIGH


def contract(pattern, left_op, right_op):
    return jnp.einsum(
        pattern, left_op, right_op, precision=three_pass, preferred_element_type=jnp.float32
    )


def digits(limbs):
    return (limbs.astype(jnp.float32) - 32768.0) * (1.0 / 32768.0)


def column_tables(half, devices):
    rows = half // (2 * devices)
    length = 2 * half
    freq = 2 * np.arange(devices * rows, dtype=np.int64)[None] + np.arange(2)[:, None]
    freq = freq.reshape(2, devices, 1, rows, 1)
    place = np.arange(half, dtype=np.int64)
    turns = freq * place % length
    wave = np.concatenate(
        [np.cos(turns * (2 * np.pi / length)), -np.sin(turns * (2 * np.pi / length))], axis=2
    )
    wave[0, 0, 1, 0] = 1.0 - 2.0 * (place % 2)
    return wave.astype(np.float32).reshape(2, half, half)


def complex_table(count, sign):
    index = np.arange(count)
    angle = (index[:, None] * index[None] % count) * (2 * np.pi / count)
    cosine, sine = np.cos(angle), sign * np.sin(angle)
    return np.stack(
        [np.stack([cosine, sine], axis=1), np.stack([-sine, cosine], axis=1)]
    ).astype(np.float32)


def rotate(real_part, imag_part, cosine, sine):
    return (real_part * cosine - imag_part * sine, real_part * sine + imag_part * cosine)


def local(a00, a01, a10, a11, b00, b01, b10, b11):
    devices = lax.axis_size("entry") * lax.axis_size("fft")
    entries = lax.axis_size("entry")
    groups = lax.axis_size("fft")
    cols = a00.shape[1]
    half = a00.shape[0] * entries
    columns = cols * groups
    length = 2 * half * columns
    rows = half // (2 * devices)
    lanes = min(LANES, cols)
    inner = cols // lanes
    outer = groups * inner
    mine = lax.axis_index("entry") * groups + lax.axis_index("fft")
    first = mine == 0

    heads = jnp.stack([digits(x) for x in (a00, a10, b00, b01)])
    tails = jnp.stack([digits(x) for x in (a01, a11, b10, b11)])
    outgoing = jnp.concatenate([heads, tails], axis=2)
    arrived = lax.all_to_all(outgoing, "entry", split_axis=0, concat_axis=0, tiled=True)
    sequence = arrived.reshape(half, 2 * cols)

    waves = column_tables(half, devices)
    outer_ahead = complex_table(outer, -1.0).reshape(2, groups, inner, 2, outer)
    outer_back = complex_table(outer, 1.0).reshape(2, outer, 2, groups, inner)
    lane_ahead = complex_table(lanes, -1.0)
    lane_back = complex_table(lanes, 1.0)
    turn = np.arange(outer)[:, None] * np.arange(lanes)[None] * (2 * np.pi / columns)
    turn_cos = np.cos(turn).astype(np.float32)[:, None, :]
    turn_sin = np.sin(turn).astype(np.float32)[:, None, :]

    pieces = []
    for parity in range(2):
        sent = contract("sp,pq->sq", waves[parity], sequence)
        sent = sent.reshape(devices, 2 * rows, 2 * cols)
        pieces.append(lax.all_to_all(sent, BOTH, split_axis=0, concat_axis=0, tiled=True))

    results = []
    for parity in range(2):
        piece = pieces[parity].reshape(entries, groups, 2, rows, 2, inner, lanes)
        real_part, imag_part = piece[:, :, 0], piece[:, :, 1]
        freq = 2 * (mine * rows + jnp.arange(rows, dtype=jnp.int32)) + parity
        if parity == 0:
            lead = first & (jnp.arange(rows) == 0)
            lead = lead[:, None, None, None]
            extra = imag_part[:, :, :1]
            imag_part = jnp.where(lead, 0.0, imag_part)
            real_part = jnp.concatenate([real_part, extra], axis=2)
            imag_part = jnp.concatenate([imag_part, jnp.zeros_like(extra)], axis=2)
            freq = jnp.concatenate([freq, jnp.full((1,), half, jnp.int32)])
        place = jnp.arange(columns, dtype=jnp.int32).reshape(groups, 1, inner, lanes)
        angle = (freq[:, None, None] * place % length).astype(jnp.float32)
        angle = angle * (2.0 * math.pi / length)
        cosine, sine = jnp.cos(angle), jnp.sin(angle)
        real_part, imag_part = rotate(
            real_part, imag_part, cosine[:, :, None], -sine[:, :, None]
        )
        both = jnp.stack([real_part, imag_part])
        step = contract("pefrnab,pfaqc->qnecrb", both, outer_ahead)
        step = jnp.stack(rotate(step[0], step[1], turn_cos, -turn_sin))
        spec = contract("pnecrb,pbqm->qnecrm", step, lane_ahead)
        left_real, left_imag = spec[0, :, :2, None], spec[1, :, :2, None]
        right_real, right_imag = spec[0, :, None, 2:], spec[1, :, None, 2:]
        mixed_real = jnp.sum(left_real * right_real - left_imag * right_imag, axis=0)
        mixed_imag = jnp.sum(left_real * right_imag + left_imag * right_real, axis=0)
        mixed = jnp.stack([mixed_real, mixed_imag])
        mixed = mixed.reshape((2, 4) + mixed.shape[3:])
        step = contract("pncrm,pmqb->qncrb", mixed, lane_back)
        step = jnp.stack(rotate(step[0], step[1], turn_cos, turn_sin))
        back = contract("pncrb,pcqfa->qnfrab", step, outer_back)
        scale = 2.0 / (length * math.sqrt(length // 2))
        back_real, back_imag = rotate(back[0], back[1], cosine * scale, sine * scale)
        if parity == 0:
            extra = back_real[:, :, rows:]
            back_real = back_real[:, :, :rows]
            back_imag = back_imag[:, :, :rows]
            back_lead = lead[:, 0]
            back_imag = jnp.where(back_lead, 0.5 * extra, back_imag)
            back_real = jnp.where(back_lead, 0.5 * back_real, back_real)
        home = jnp.stack([back_real, back_imag], axis=2)
        home = home.reshape(devices, 2 * rows, cols)
        home = lax.all_to_all(home, BOTH, split_axis=0, concat_axis=0, tiled=True)
        results.append(contract("sp,sq->pq", waves[parity], home.reshape(half, cols)))
    even, odd = results
    return jnp.stack([even + odd, even - odd]).reshape(1, 2 * half, cols)


def solution(mesh):
    return jax.shard_map(
        local,
        mesh=mesh,
        in_specs=(P("entry", "fft"),) * 8,
        out_specs=P("entry", None, "fft"),
        check_vma=False,
    )
```
